128 devices in a mesh: blk: 32 (over y, z, x_lo), head: 4 (over x_hi, core).
Axes of the slice: x: 4 (x_hi: 2, x_lo: 2; x = x_hi * 2 + x_lo), y: 4, z: 4, core: 2. Of those that a mesh axis runs over, the one named last changes fastest.
Arguments:
- hidden_states: bfloat16 [16384, 4096], P('blk'), may hold values from -16 to 16
- w_query: bfloat16 [4096, 4096], P(None, 'head'), may hold values from -0.09375 to 0.09375
- key_matrix: bfloat16 [4096, 1024], P(None, 'head'), may hold values from -0.09375 to 0.09375
- value_matrix: bfloat16 [4096, 1024], P(None, 'head'), may hold values from -0.09375 to 0.09375
- w_out: bfloat16 [4096, 4096], P('head'), may hold values from -0.125 to 0.125
Outputs:
- attn_out: bfloat16 [16384, 4096], P('blk', 'head')
The draws below stay inside these ranges and needn't reach their ends.
All inputs are finite; a program needn't handle non-finite values.
Results may differ from the reference program's by a relative error of at most 0.012.
Values may be sent and summed in bfloat16 or wider, within the bound.
A program may use at most 128 MiB of HBM per device.

```python
import jax
import jax.numpy as jnp
from jax import lax

MODEL_WIDTH = 4096
QUERY_HEADS = 32
KEY_VALUE_HEADS = 8
HEAD_SIZE = 128
BLK = 512
SEQ = 16384


def draw_hidden_states(key, part):
    key = jax.random.fold_in(key, 7)
    value_rows = jnp.clip(jax.random.normal(key, (SEQ, MODEL_WIDTH), jnp.float32), -6.0, 6.0)
    return value_rows.astype(jnp.bfloat16)


def raised(values, stream_key, source, target, parts, factor):
    owner, partner = [(jnp.arange(values.shape[dim]) // (values.shape[dim] // parts)).reshape([-1 if axis == dim else 1 for axis in range(values.ndim)]) for dim in (source, target)]
    chosen = jax.random.permutation(stream_key, parts)[partner]
    strong = (owner == chosen) | (owner == (partner + parts // 2) % parts)
    return jnp.where(strong, factor * values, values)


def level_of(stream_key, dims, split, least, top_value):
    level = 1.0
    for dim, shards_of in split:
        heights = jax.random.uniform(jax.random.fold_in(jax.random.fold_in(stream_key, 6), dim), (shards_of,), jnp.float32, least / len(split), top_value / len(split))
        level = level * jnp.repeat(jnp.exp(heights), dims[dim] // shards_of).reshape((-1,) + (1,) * (len(dims) - 1 - dim))
    return level


def centred(rng, dims, scale, limit, pieces=(), held_as=jnp.bfloat16):
    array = scale * jax.random.normal(rng, dims, jnp.float32)
    if pieces:
        array = array * level_of(rng, dims, pieces, -0.22, 0.18)
    return jnp.clip(array, -limit, limit).astype(held_as)


def noise_with(rng, shape, scale, most, shards, heavy, kind=jnp.bfloat16):
    array = scale * jax.random.normal(rng, shape, jnp.float32)
    if shards:
        array = array * level_of(rng, shape, shards, -0.22, 0.18)
    return jnp.clip(raised(array, jax.random.fold_in(rng, 3), *heavy), -most, most).astype(kind)


def setup_inputs(seed: int = 0) -> dict:
    seeds = jax.random.split(jax.random.key(seed), 6)
    hidden_states = draw_hidden_states(jax.random.fold_in(seeds[5], 71), 0)
    w_query = centred(seeds[1], (MODEL_WIDTH, QUERY_HEADS * HEAD_SIZE), MODEL_WIDTH ** -0.5, 0.09375, ((1, 4),))
    key_matrix = centred(seeds[2], (MODEL_WIDTH, KEY_VALUE_HEADS * HEAD_SIZE), MODEL_WIDTH ** -0.5, 0.09375, ((1, 4),))
    value_matrix = centred(seeds[3], (MODEL_WIDTH, KEY_VALUE_HEADS * HEAD_SIZE), MODEL_WIDTH ** -0.5, 0.09375, ((1, 4),))
    w_out = noise_with(seeds[4], (QUERY_HEADS * HEAD_SIZE, MODEL_WIDTH), (QUERY_HEADS * HEAD_SIZE) ** -0.5, 0.125, ((0, 4),), (0, 1, 4, 2.0))
    return dict(hidden_states=hidden_states, w_query=w_query, key_matrix=key_matrix, value_matrix=value_matrix, w_out=w_out)


def apply_rotation(value_rows, token_positions, heads):
    token_rows = value_rows.shape[0]
    grid = value_rows.reshape(token_rows, heads, HEAD_SIZE)
    half = HEAD_SIZE // 2
    freqs = 500000.0 ** (-2.0 * jnp.arange(half, dtype=jnp.float32) / HEAD_SIZE)
    angle = token_positions[:, None] * freqs[None, :]
    cosine = jnp.cos(angle)[:, None, :]
    sine = jnp.sin(angle)[:, None, :]
    first = grid[:, :, :half]
    second = grid[:, :, half:]
    turned = jnp.concatenate([first * cosine - second * sine, second * cosine + first * sine], axis=2)
    return turned.reshape(token_rows, heads * HEAD_SIZE).astype(jnp.bfloat16)

def project_pairs(tokens, key_matrix, value_matrix, token_positions):
    key_rows = jnp.dot(tokens, key_matrix, preferred_element_type=jnp.float32)
    value_rows = jnp.dot(tokens, value_matrix, preferred_element_type=jnp.float32).astype(jnp.bfloat16)
    return (apply_rotation(key_rows, token_positions, KEY_VALUE_HEADS), value_rows)

def attend(query_rows, key_rows, value_rows, leading_block_keys, leading_block_values, anchor_on):
    token_rows = query_rows.shape[0]
    repeat_heads = QUERY_HEADS // KEY_VALUE_HEADS
    query_layout = query_rows.reshape(token_rows, KEY_VALUE_HEADS, repeat_heads, HEAD_SIZE).astype(jnp.float32)
    joined_keys = jnp.concatenate([leading_block_keys, key_rows], axis=0).reshape(2 * token_rows, KEY_VALUE_HEADS, HEAD_SIZE).astype(jnp.float32)
    joined_values = jnp.concatenate([leading_block_values, value_rows], axis=0).reshape(2 * token_rows, KEY_VALUE_HEADS, HEAD_SIZE).astype(jnp.float32)
    scores = jnp.einsum('rgph,sgh->gprs', query_layout, joined_keys) / jnp.sqrt(jnp.float32(HEAD_SIZE))
    row_index = jnp.arange(token_rows)[:, None]
    col_index = jnp.arange(2 * token_rows)[None, :]
    visible = jnp.where(col_index < token_rows, anchor_on, col_index - token_rows <= row_index)
    scores = jnp.where(visible[None, None], scores, -jnp.inf)
    top = lax.optimization_barrier(jnp.max(scores, axis=3, keepdims=True))
    expo = jnp.exp(scores - top)
    weights = (expo / lax.optimization_barrier(jnp.sum(expo, axis=3, keepdims=True))).astype(jnp.bfloat16)
    context = jnp.einsum('gprs,sgh->rgph', weights.astype(jnp.float32), joined_values)
    return context.reshape(token_rows, QUERY_HEADS * HEAD_SIZE).astype(jnp.bfloat16)

def reference(hidden_states, w_query, key_matrix, value_matrix, w_out):
    anchor_pos = jnp.arange(BLK, dtype=jnp.float32)
    leading_block_keys, leading_block_values = project_pairs(hidden_states[:BLK], key_matrix, value_matrix, anchor_pos)

    def one_block(index):
        start = index * BLK
        tokens = lax.dynamic_slice_in_dim(hidden_states, start, BLK, 0)
        token_positions = (start + jnp.arange(BLK, dtype=jnp.int32)).astype(jnp.float32)
        query_rows = apply_rotation(jnp.dot(tokens, w_query, preferred_element_type=jnp.float32), token_positions, QUERY_HEADS)
        key_rows, value_rows = project_pairs(tokens, key_matrix, value_matrix, token_positions)
        context = attend(query_rows, key_rows, value_rows, leading_block_keys, leading_block_values, index > 0)
        return jnp.dot(context, w_out, preferred_element_type=jnp.float32).astype(jnp.bfloat16)
    blocks = lax.map(one_block, jnp.arange(SEQ // BLK, dtype=jnp.int32))
    return blocks.reshape(SEQ, MODEL_WIDTH)
```

```python
import jax
import jax.numpy as jnp
import numpy as np
from jax import lax
from jax.experimental import pallas as pl
from jax.experimental.pallas import tpu as pltpu
from jax.sharding import PartitionSpec as P

HEAD = 128
ROWS = 512
WIDTH = 4096
TILE = 128
TILES = ROWS // TILE
CHUNKS = 2
CROWS = ROWS // CHUNKS
PIECE = CROWS // 16
BODY = 256
MESH = pl.DeviceIdType.MESH
LOW = -1e30
F32 = jnp.float32
BF16 = jnp.bfloat16


def rotary_tables(blocks):
    half = HEAD // 2
    freqs = 500000.0 ** (-2.0 * np.arange(half) / HEAD)
    rows = np.arange(ROWS)[:, None] * freqs[None, :]
    starts = (np.arange(blocks) * ROWS)[:, None] * freqs[None, :]

    def both(x):
        return np.concatenate([x, x], axis=1).astype(np.float32)

    return (
        np.stack([both(np.cos(rows)), both(np.sin(rows))]),
        np.stack([both(np.cos(starts)), both(np.sin(starts))], axis=1),
    )


def dot(a, b):
    return jnp.dot(a, b, preferred_element_type=F32)


def dot_t(a, b):
    return lax.dot_general(a, b, (((1,), (1,)), ((), ())), preferred_element_type=F32)


def kernel(
    hid, wq, wk, wv, wo, row_tab, start_tab, out,
    hid_v, wq_v, wkv_v, wo_a, wo_b, rows_v, start_v, cos_v, sin_v,
    kvl, kva, q_v, vl_aug, va_aug, ol, ml, ctx, ctx_sib, acc_r, acc_l, sbuf, rbuf, obuf,
    hid_sem, wkv_sem, tab_sem, wq_sem, woa_sem, wob_send, wob_recv,
    sc_send, sc_recv, xl_send, xl_recv, ag_send, ag_recv,
    ctx_send, ctx_recv, x_send, x_recv, out_sem, own_sem,
):
    blk = lax.axis_index("blk")
    head = lax.axis_index("head")
    xl = lax.rem(blk, 2)
    pos = blk // 2
    y, z = pos // 4, lax.rem(pos, 4)
    xh, core = head // 2, lax.rem(head, 2)

    def plane(dy, dz):
        return ((lax.rem(y + dy, 4) * 4 + lax.rem(z + dz, 4)) * 2 + xl, head)

    peers = [plane(dy, dz) for dy in range(4) for dz in range(4) if (dy, dz) != (0, 0)]
    xl_peer = (pos * 2 + 1 - xl, head)
    sibling = (blk, xh * 2 + 1 - core)
    far_head = (1 - xh) * 2 + core
    far = (blk, far_head)

    barrier = pltpu.get_barrier_semaphore()
    friends = peers + [xl_peer, sibling, far]
    for friend in friends:
        pl.semaphore_signal(barrier, inc=1, device_id=friend, device_id_type=MESH)

    hid_cp = [
        pltpu.make_async_copy(
            hid.at[pl.ds(i * CROWS, CROWS)], hid_v.at[pl.ds(i * CROWS, CROWS)], hid_sem.at[i]
        )
        for i in range(CHUNKS)
    ]
    wk_cp = pltpu.make_async_copy(wk, wkv_v.at[:, pl.ds(0, 256)], wkv_sem.at[0])
    wv_cp = pltpu.make_async_copy(wv, wkv_v.at[:, pl.ds(256, 256)], wkv_sem.at[1])
    rows_cp = pltpu.make_async_copy(row_tab, rows_v, tab_sem.at[0])
    start_cp = pltpu.make_async_copy(start_tab, start_v, tab_sem.at[1])
    wq_cp = [
        pltpu.make_async_copy(wq.at[:, pl.ds(n * 256, 256)], wq_v.at[n], wq_sem.at[n])
        for n in range(4)
    ]
    woa_cp = [
        pltpu.make_async_copy(
            wo.at[:, pl.ds(pl.multiple_of(h * 1024, 1024), 1024)], wo_a.at[i], woa_sem.at[i]
        )
        for i, h in enumerate((far_head, head))
    ]
    hid_cp[0].start()
    wk_cp.start()
    wv_cp.start()
    start_cp.start()
    rows_cp.start()
    for cp in hid_cp[1:] + wq_cp:
        cp.start()

    start_cp.wait()
    rows_cp.wait()
    sign = jnp.where(lax.broadcasted_iota(jnp.int32, (TILE, HEAD), 1) < HEAD // 2, -1.0, 1.0)
    c0 = start_v[blk, 0:1, :]
    s0 = start_v[blk, 1:2, :]

    def make_tables(i, carry):
        rows = pl.ds(pl.multiple_of(i * TILE, TILE), TILE)
        cr, sr = rows_v[0, rows, :], rows_v[1, rows, :]
        cos_v[rows, :] = c0 * cr - s0 * sr
        sin_v[rows, :] = (s0 * cr + c0 * sr) * sign
        return carry

    lax.fori_loop(0, TILES, make_tables, 0)
    scale = float(np.log2(np.e) / np.sqrt(HEAD))

    def turn(x, c, s):
        return x * c + pltpu.roll(x, HEAD // 2, 1) * s

    def scatter(ch, i, target):
        rows = pl.ds(pl.multiple_of(ch * CROWS + i * PIECE, PIECE), PIECE)
        return pltpu.make_async_remote_copy(
            src_ref=kvl.at[rows], dst_ref=kva.at[rows], send_sem=sc_send.at[ch],
            recv_sem=sc_recv.at[ch], device_id=target, device_id_type=MESH,
        )

    def own_piece(ch):
        return pl.ds(pl.multiple_of(ch * CROWS + pos * PIECE, PIECE), PIECE)

    def forward(ch):
        rows = own_piece(ch)
        return pltpu.make_async_remote_copy(
            src_ref=kva.at[rows], dst_ref=kva.at[rows], send_sem=xl_send.at[ch],
            recv_sem=xl_recv.at[ch], device_id=xl_peer, device_id_type=MESH,
        )

    def gather(ch, target):
        rows = own_piece(ch)
        return pltpu.make_async_remote_copy(
            src_ref=kva.at[rows], dst_ref=kva.at[rows], send_sem=ag_send.at[ch],
            recv_sem=ag_recv.at[ch], device_id=target, device_id_type=MESH,
        )

    def own_copy(ch):
        rows = pl.ds(ch * CROWS, PIECE)
        return pltpu.make_async_copy(kvl.at[rows], kva.at[rows], own_sem.at[ch])

    def scatter_chunk(ch):
        @pl.when(blk == 0)
        def _():
            own_copy(ch).start()
            for dy in range(4):
                for dz in range(4):
                    if (dy, dz) != (0, 0):
                        scatter(ch, dy * 4 + dz, (jnp.int32((dy * 4 + dz) * 2), head)).start()

    def relay(ch, side):
        @pl.when(xl == side)
        def _():
            if side == 0:
                @pl.when(blk == 0)
                def _():
                    own_copy(ch).wait()

                @pl.when(blk != 0)
                def _():
                    scatter(ch, 0, sibling).wait_recv()

                forward(ch).start()
            else:
                forward(ch).wait_recv()
            for target in peers:
                gather(ch, target).start()

    wk_cp.wait()
    wv_cp.wait()
    for i in range(CHUNKS):
        hid_cp[i].wait()
        rows = pl.ds(i * CROWS, CROWS)
        kv = dot(hid_v[rows, :], wkv_v[...])
        c, s = cos_v[rows, :], sin_v[rows, :]
        for g in range(2):
            cols = slice(g * HEAD, (g + 1) * HEAD)
            kvl[rows, cols] = turn(kv[:, cols], c, s).astype(BF16)
        kvl[rows, 256:512] = kv[:, 256:512].astype(BF16)
        if i == 0:
            pl.semaphore_wait(barrier, len(friends))
        scatter_chunk(i)
    for g in range(2):
        vl_aug[g, :, 0:HEAD] = kvl[:, 256 + g * HEAD : 256 + (g + 1) * HEAD]
        vl_aug[g, :, HEAD:] = jnp.ones((ROWS, HEAD), BF16)
        va_aug[g, :, HEAD:] = jnp.ones((ROWS, HEAD), BF16)

    other = 1 - core
    wob_cp = [
        pltpu.make_async_remote_copy(
            src_ref=wo.at[:, pl.ds(pl.multiple_of(h * 1024, 1024), 1024)], dst_ref=wo_b.at[i],
            send_sem=wob_send.at[i], recv_sem=wob_recv.at[i],
            device_id=sibling, device_id_type=MESH,
        )
        for i, h in enumerate(((1 - xh) * 2 + other, xh * 2 + other))
    ]
    for cp in woa_cp + wob_cp:
        cp.start()

    for n in range(4):
        wq_cp[n].wait()
        g, j0 = n // 2, (n % 2) * 2

        def q_rows(m, carry, n=n, g=g, j0=j0):
            rows = pl.ds(pl.multiple_of(m * 256, 256), 256)
            x = dot(hid_v[rows, :], wq_v[n])
            c, s = cos_v[rows, :] * scale, sin_v[rows, :] * scale
            for j in range(2):
                turned = turn(x[:, j * HEAD : (j + 1) * HEAD], c, s).astype(BF16)
                for tt in range(2):
                    q_v[(2 * m + tt) * 2 + g, pl.ds((j0 + j) * TILE, TILE), :] = turned[
                        tt * TILE : (tt + 1) * TILE
                    ]
            return carry

        lax.fori_loop(0, 2, q_rows, 0)
        if n == 2:
            relay(0, 0)
    relay(1, 0)

    def local_tile(t):
        keys = (t + 1) * TILE
        diag = (
            lax.broadcasted_iota(jnp.int32, (BODY, keys), 1) - t * TILE
            <= lax.rem(lax.broadcasted_iota(jnp.int32, (BODY, keys), 0), TILE)
        )
        for g in range(2):
            def body(b, carry, g=g):
                rows = pl.ds(pl.multiple_of(b * BODY, BODY), BODY)
                s = dot_t(q_v[t * 2 + g, rows, :], kvl[0:keys, g * HEAD : (g + 1) * HEAD])
                s = jnp.where(diag, s, LOW)
                top = jnp.max(s, axis=1, keepdims=True)
                p = jnp.exp2(s - top).astype(BF16)
                ol[t * 2 + g, rows, :] = dot(p, vl_aug[g, 0:keys, :])
                ml[t * 2 + g, rows, :] = jnp.broadcast_to(top, (BODY, HEAD))
                return carry

            lax.fori_loop(0, ROWS // BODY, body, 0)

    local_tile(0)
    local_tile(1)
    relay(0, 1)
    local_tile(2)
    relay(1, 1)
    local_tile(3)

    got = pl.ds(0, 15 * PIECE)
    for ch in range(CHUNKS):
        pltpu.make_async_copy(kva.at[got], kva.at[got], ag_recv.at[ch]).wait()
    for g in range(2):
        va_aug[g, :, 0:HEAD] = kva[:, 256 + g * HEAD : 256 + (g + 1) * HEAD]

    def ctx_copy(t, g):
        cols = pl.ds(g * 512, 512)
        return pltpu.make_async_remote_copy(
            src_ref=ctx.at[t, :, cols], dst_ref=ctx_sib.at[t, :, cols],
            send_sem=ctx_send.at[t, g], recv_sem=ctx_recv.at[t, g],
            device_id=sibling, device_id_type=MESH,
        )

    def x_copy(t):
        return pltpu.make_async_remote_copy(
            src_ref=sbuf.at[t], dst_ref=rbuf.at[t], send_sem=x_send.at[t],
            recv_sem=x_recv.at[t], device_id=far, device_id_type=MESH,
        )

    has_anchor = blk > 0
    for t in range(TILES):
        for g in range(2):
            for b in range(ROWS // BODY):
                rows = slice(b * BODY, (b + 1) * BODY)
                s = dot_t(q_v[t * 2 + g, rows, :], kva[:, g * HEAD : (g + 1) * HEAD])
                before = ml[t * 2 + g, rows, :][:, 0:1]
                both = jnp.maximum(jnp.max(s, axis=1, keepdims=True), before)
                top = jnp.where(has_anchor, both, before)
                p = jnp.exp2(s - jnp.where(has_anchor, both, -LOW)).astype(BF16)
                o = dot(p, va_aug[g]) + ol[t * 2 + g, rows, :] * jnp.exp2(before - top)
                res = (o[:, 0:HEAD] / o[:, HEAD:]).astype(BF16)
                for j in range(BODY // TILE):
                    col = (g * 4 + b * (BODY // TILE) + j) * HEAD
                    ctx[t, :, col : col + HEAD] = res[j * TILE : (j + 1) * TILE]
            ctx_copy(t, g).start()
        if t == 0:
            for cp in woa_cp:
                cp.wait()

        def own_part(n, carry, t=t):
            cols = pl.ds(pl.multiple_of(n * 256, 256), 256)
            acc_r[:, cols] = dot(ctx[t], wo_a[0, :, cols])
            acc_l[t, :, cols] = dot(ctx[t], wo_a[1, :, cols])
            return carry

        lax.fori_loop(0, 4, own_part, 0)
        if t == 0:
            for cp in wob_cp:
                cp.wait_recv()
        for g in range(2):
            ctx_copy(t, g).wait_recv()

        def far_part(n, carry, t=t):
            cols = pl.ds(pl.multiple_of(n * 256, 256), 256)
            sbuf[t, :, cols] = (acc_r[:, cols] + dot(ctx_sib[t], wo_b[0, :, cols])).astype(BF16)
            return carry

        lax.fori_loop(0, 4, far_part, 0)
        x_copy(t).start()

        def near_part(n, carry, t=t):
            cols = pl.ds(pl.multiple_of(n * 256, 256), 256)
            acc_l[t, :, cols] += dot(ctx_sib[t], wo_b[1, :, cols])
            return carry

        lax.fori_loop(0, 4, near_part, 0)

    out_cp = [
        pltpu.make_async_copy(obuf.at[t], out.at[pl.ds(t * TILE, TILE)], out_sem.at[t])
        for t in range(TILES)
    ]
    for t in range(TILES):
        x_copy(t).wait_recv()
        obuf[t] = (acc_l[t] + rbuf[t].astype(F32)).astype(BF16)
        out_cp[t].start()

    for cp in wob_cp:
        cp.wait_send()
    for ch in range(CHUNKS):
        @pl.when(blk == 0)
        def _(ch=ch):
            pltpu.make_async_copy(kvl.at[got], kvl.at[got], sc_send.at[ch]).wait()

        @pl.when(xl == 0)
        def _(ch=ch):
            forward(ch).wait_send()

        pltpu.make_async_copy(kva.at[got], kva.at[got], ag_send.at[ch]).wait()
    for t in range(TILES):
        for g in range(2):
            ctx_copy(t, g).wait_send()
        x_copy(t).wait_send()
        out_cp[t].wait()


def local(hidden_states, w_query, key_matrix, value_matrix, w_out):
    row_tab, start_tab = rotary_tables(32)
    any_spec = pl.BlockSpec(memory_space=pl.ANY)
    dma = pltpu.SemaphoreType.DMA
    return pl.pallas_call(
        kernel,
        out_shape=jax.ShapeDtypeStruct((ROWS, 1024), BF16),
        in_specs=[any_spec] * 7,
        out_specs=any_spec,
        scratch_shapes=[
            pltpu.VMEM((ROWS, WIDTH), BF16),
            pltpu.VMEM((4, WIDTH, 256), BF16),
            pltpu.VMEM((WIDTH, 512), BF16),
            pltpu.VMEM((2, 1024, 1024), BF16),
            pltpu.VMEM((2, 1024, 1024), BF16),
            pltpu.VMEM((2, ROWS, HEAD), F32),
            pltpu.VMEM((32, 2, HEAD), F32),
            pltpu.VMEM((ROWS, HEAD), F32),
            pltpu.VMEM((ROWS, HEAD), F32),
            pltpu.VMEM((ROWS, 512), BF16),
            pltpu.VMEM((ROWS, 512), BF16),
            pltpu.VMEM((TILES * 2, 4 * TILE, HEAD), BF16),
            pltpu.VMEM((2, ROWS, 2 * HEAD), BF16),
            pltpu.VMEM((2, ROWS, 2 * HEAD), BF16),
            pltpu.VMEM((TILES * 2, 4 * TILE, 2 * HEAD), F32),
            pltpu.VMEM((TILES * 2, 4 * TILE, HEAD), F32),
            pltpu.VMEM((TILES, TILE, 1024), BF16),
            pltpu.VMEM((TILES, TILE, 1024), BF16),
            pltpu.VMEM((TILE, 1024), F32),
            pltpu.VMEM((TILES, TILE, 1024), F32),
            pltpu.VMEM((TILES, TILE, 1024), BF16),
            pltpu.VMEM((TILES, TILE, 1024), BF16),
            pltpu.VMEM((TILES, TILE, 1024), BF16),
            dma((CHUNKS,)), dma((2,)), dma((2,)), dma((4,)), dma((2,)), dma((2,)), dma((2,)),
            dma((CHUNKS,)), dma((CHUNKS,)), dma((CHUNKS,)), dma((CHUNKS,)),
            dma((CHUNKS,)), dma((CHUNKS,)),
            dma((TILES, 2)), dma((TILES, 2)), dma((TILES,)), dma((TILES,)), dma((TILES,)),
            dma((CHUNKS,)),
        ],
        compiler_params=pltpu.CompilerParams(
            collective_id=0, has_side_effects=True, vmem_limit_bytes=60 * 2**20
        ),
        name="layer",
    )(
        hidden_states, w_query, key_matrix, value_matrix, w_out,
        jnp.asarray(row_tab), jnp.asarray(start_tab),
    )


def solution(mesh):
    in_specs = (P("blk", None), P(None, "head"), P(None, "head"), P(None, "head"), P("head", None))
    out_specs = P("blk", "head")
    return jax.shard_map(local, mesh=mesh, in_specs=in_specs, out_specs=out_specs, check_vma=False)
```

```python
import jax
import jax.numpy as jnp
import numpy as np
from jax import lax
from jax.experimental import pallas as pl
from jax.experimental.pallas import tpu as pltpu
from jax.sharding import PartitionSpec as P

HEAD = 128
ROWS = 512
WIDTH = 4096
TILE = 128
TILES = ROWS // TILE
CHUNKS = 2
CROWS = ROWS // CHUNKS
PIECE = CROWS // 8
BODY = 256
MESH = pl.DeviceIdType.MESH
LOW = -1e30
F32 = jnp.float32
BF16 = jnp.bfloat16


def rotary_tables(blocks):
    freqs = 500000.0 ** (-2.0 * np.arange(HEAD // 2) / HEAD)

    def table(tokens):
        angle = tokens[..., None] * freqs
        both = [np.concatenate([f(angle)] * 2, axis=-1) for f in (np.cos, np.sin)]
        return np.stack(both, axis=-3).astype(np.float32)

    return table(np.arange(blocks * ROWS // 16).reshape(blocks, -1) * 16.0), table(np.arange(16.0))


def dot(a, b):
    return jnp.dot(a, b, preferred_element_type=F32)


def dot_t(a, b):
    return lax.dot_general(a, b, (((1,), (1,)), ((), ())), preferred_element_type=F32)


def kernel(
    hid, wq, wk, wv, wo, coarse_tab, fine_tab, out,
    hid_v, wq_v, wkv_v, wo_a, wo_b, coarse, fine, cos_v, sin_v,
    kv_acc, kvl, kva, stage, q_v, vl_aug, va_aug, ol, ml, ctx, ctx_sib, acc_r, acc_l, sbuf, rbuf,
    hid_sem, wkv_sem, tab_sem, wq_sem, woa_sem, wob_send, wob_recv,
    first_send, aside_send, mine_recv, ring_send, fwd_send, rest_send, home_send, rest_recv,
    ctx_send, ctx_recv, x_send, x_recv, own_sem,
):
    blk = lax.axis_index("blk")
    head = lax.axis_index("head")
    xl = lax.rem(blk, 2)
    pos = blk // 2
    y, z = pos // 4, lax.rem(pos, 4)
    xh, core = head // 2, lax.rem(head, 2)

    def along(part, d):
        if part == 0:
            return (lax.rem(y + d, 4) * 4 + z) * 2 + xl
        return (y * 4 + lax.rem(z + d, 4)) * 2 + xl

    rings = [[along(part, d) for d in (1, 2, 3)] for part in range(2)]
    xl_peer = pos * 2 + 1 - xl
    zero, one = xh * 2, xh * 2 + 1
    sibling = (blk, xh * 2 + 1 - core)
    far_head = (1 - xh) * 2 + core
    far = (blk, far_head)

    barrier = pltpu.get_barrier_semaphore()
    friends = [(b, h) for b in rings[0] + rings[1] for h in (zero, one)]
    friends += [(xl_peer, head), sibling, far]
    for friend in friends:
        pl.semaphore_signal(barrier, inc=1, device_id=friend, device_id_type=MESH)

    hid_cp = [
        pltpu.make_async_copy(
            hid.at[pl.ds(0, CROWS), pl.ds(d * 2048, 2048)],
            hid_v.at[pl.ds(0, CROWS), pl.ds(d * 2048, 2048)],
            hid_sem.at[d],
        )
        for d in range(2)
    ]
    later_cp = pltpu.make_async_copy(
        hid.at[pl.ds(CROWS, CROWS)], hid_v.at[pl.ds(CROWS, CROWS)], hid_sem.at[2]
    )
    half = WIDTH // 2
    wkv_cp = [
        pltpu.make_async_copy(
            w.at[pl.ds(d * half, half)],
            wkv_v.at[pl.ds(d * half, half), pl.ds(i * 256, 256)],
            wkv_sem.at[d, i],
        )
        for d in range(2)
        for i, w in enumerate((wk, wv))
    ]
    tab_cp = [
        pltpu.make_async_copy(coarse_tab.at[blk], coarse, tab_sem.at[0]),
        pltpu.make_async_copy(fine_tab, fine, tab_sem.at[1]),
    ]
    wq_cp = [
        pltpu.make_async_copy(wq.at[:, pl.ds(n * 512, 512)], wq_v.at[n], wq_sem.at[n])
        for n in range(2)
    ]
    woa_cp = [
        pltpu.make_async_copy(
            wo.at[:, pl.ds(pl.multiple_of(h * 1024, 1024), 1024)], wo_a.at[i], woa_sem.at[i]
        )
        for i, h in enumerate((far_head, head))
    ]
    first_half = [hid_cp[0], wkv_cp[0], wkv_cp[1]]
    second_half = [hid_cp[1], wkv_cp[2], wkv_cp[3]]
    for cp in tab_cp + first_half + second_half + [later_cp]:
        cp.start()
    def make_tables():
        lane = lax.broadcasted_iota(jnp.int32, (16, HEAD), 1)
        sign = jnp.where(lane < HEAD // 2, -1.0, 1.0)
        cf, sf = fine[0], fine[1]

        def step(i, carry):
            ca, sa = coarse[0, pl.ds(i, 1), :], coarse[1, pl.ds(i, 1), :]
            rows = pl.ds(pl.multiple_of(i * 16, 16), 16)
            cos_v[rows, :] = ca * cf - sa * sf
            sin_v[rows, :] = (sa * cf + ca * sf) * sign
            return carry

        lax.fori_loop(0, ROWS // 16, step, 0, unroll=4)

    scale = float(np.log2(np.e) / np.sqrt(HEAD))

    def turn(x, c, s):
        return x * c + pltpu.roll(x, HEAD // 2, 1) * s

    lines = (y, z)
    held = (stage, kva)

    def piece(ch, part, j):
        return pl.ds(pl.multiple_of(ch * CROWS + (part * 4 + j) * PIECE, PIECE), PIECE)

    def push(src, dst, ch, part, j, send_sem, recv_sem, target):
        rows = piece(ch, part, j)
        return pltpu.make_async_remote_copy(
            src_ref=src.at[rows], dst_ref=dst.at[rows], send_sem=send_sem, recv_sem=recv_sem,
            device_id=target, device_id_type=MESH,
        )

    def own_copy(ch, part):
        rows = piece(ch, part, 0)
        return pltpu.make_async_copy(kvl.at[rows], kva.at[rows], own_sem.at[ch, part])

    def aside(ch, part):
        return push(
            kvl, stage, ch, part, 0, aside_send.at[ch, part], mine_recv.at[ch, part, 0], sibling
        )

    def first(ch, part, d, grp):
        return push(
            kvl, held[grp], ch, part, d, first_send.at[ch], mine_recv.at[ch, part, grp],
            (rings[part][d - 1], one),
        )

    def forward(ch, part, grp):
        return push(
            held[grp], held[grp], ch, part, lines[part], fwd_send.at[ch, part, grp],
            mine_recv.at[ch, part, grp], (xl_peer, one),
        )

    def across(ch, part, d, grp):
        return push(
            held[grp], held[grp], ch, part, lines[part], ring_send.at[ch, part, grp],
            mine_recv.at[ch, part, grp], (rings[1 - part][d - 1], one),
        )

    def rest(ch, part, d, grp):
        return push(
            held[grp], kva, ch, part, lines[part], rest_send.at[ch, grp], rest_recv.at[ch],
            (rings[part][d - 1], (zero, one)[grp]),
        )

    def home(ch, part):
        return push(
            stage, kva, ch, part, lines[part], home_send.at[ch, part], rest_recv.at[ch], sibling
        )

    def scatter_chunk(ch):
        for grp in range(2):
            @pl.when(jnp.logical_and(blk == 0, core == grp))
            def _(grp=grp):
                for part in range(2):
                    for d in (1, 2, 3):
                        first(ch, part, d, grp).start()
                for part in range(2):
                    if grp == 0:
                        aside(ch, part).start()
                    else:
                        own_copy(ch, part).start()

    def relay_part(ch, part, early):
        at_root = lines[1 - part] == 0

        @pl.when(at_root if early else jnp.logical_not(at_root))
        def _():
            forward(ch, part, 0).wait_recv()
            if early:
                @pl.when(blk == 0)
                def _():
                    own_copy(ch, part).wait()

                @pl.when(blk != 0)
                def _():
                    forward(ch, part, 1).wait_recv()
            else:
                forward(ch, part, 1).wait_recv()
            if early:
                for grp in range(2):
                    @pl.when(xl == 0)
                    def _(grp=grp):
                        forward(ch, part, grp).start()

                    for d in (1, 2, 3):
                        across(ch, part, d, grp).start()
            else:
                send_rest(ch, part)

    def send_rest(ch, part):
        for grp in range(2):
            for d in (1, 2, 3):
                rest(ch, part, d, grp).start()
        home(ch, part).start()

    def root_rest(side):
        for part in range(2):
            mine = jnp.logical_and(lines[1 - part] == 0, xl == side)

            @pl.when(jnp.logical_and(mine, core == 1))
            def _(part=part):
                for ch in range(CHUNKS):
                    send_rest(ch, part)

    def relay(ch, side, early):
        @pl.when(jnp.logical_and(xl == side, core == 1))
        def _():
            for part in range(2):
                relay_part(ch, part, early)

    for cp in first_half:
        cp.wait()
    for i in range(CHUNKS):
        rows = pl.ds(i * CROWS, CROWS)
        if i == 0:
            kv_acc[...] = dot(hid_v[rows, 0:half], wkv_v[0:half, :])
            for cp in second_half:
                cp.wait()
            for cp in wq_cp:
                cp.start()
            kv_acc[...] += dot(hid_v[rows, half:], wkv_v[half:, :])
            for cp in tab_cp:
                cp.wait()
            make_tables()
            kv = kv_acc[...]
        else:
            later_cp.wait()
            kv = dot(hid_v[rows, :], wkv_v[...])
        c, s = cos_v[rows, :], sin_v[rows, :]
        for g in range(2):
            cols = slice(g * HEAD, (g + 1) * HEAD)
            kvl[rows, cols] = turn(kv[:, cols], c, s).astype(BF16)
        kvl[rows, 256:512] = kv[:, 256:512].astype(BF16)
    pl.semaphore_wait(barrier, len(friends))
    for ch in range(CHUNKS):
        scatter_chunk(ch)
    for g in range(2):
        vl_aug[g, :, 0:HEAD] = kvl[:, 256 + g * HEAD : 256 + (g + 1) * HEAD]
        vl_aug[g, :, HEAD:] = jnp.ones((ROWS, HEAD), BF16)
        va_aug[g, :, HEAD:] = jnp.ones((ROWS, HEAD), BF16)

    other = 1 - core
    wob_cp = [
        pltpu.make_async_remote_copy(
            src_ref=wo.at[:, pl.ds(pl.multiple_of(h * 1024, 1024), 1024)], dst_ref=wo_b.at[i],
            send_sem=wob_send.at[i], recv_sem=wob_recv.at[i],
            device_id=sibling, device_id_type=MESH,
        )
        for i, h in enumerate(((1 - xh) * 2 + other, xh * 2 + other))
    ]
    for cp in woa_cp + wob_cp:
        cp.start()

    relay(0, 0, True)
    relay(1, 0, True)
    for n in range(4):
        g, m = n // 2, n % 2
        if m == 0:
            wq_cp[g].wait()
        x = dot(hid_v[m * 256 : (m + 1) * 256, :], wq_v[g])
        rows = slice(m * 256, (m + 1) * 256)
        c, s = cos_v[rows, :] * scale, sin_v[rows, :] * scale
        for j in range(4):
            turned = turn(x[:, j * HEAD : (j + 1) * HEAD], c, s).astype(BF16)
            for tt in range(2):
                q_v[(2 * m + tt) * 2 + g, j * TILE : (j + 1) * TILE, :] = turned[
                    tt * TILE : (tt + 1) * TILE
                ]
        if n == 1:
            root_rest(0)
        if n == 2:
            relay(0, 1, True)
            relay(1, 1, True)
            relay(0, 0, False)
            relay(1, 0, False)
        if n == 3:
            root_rest(1)

    diag = lax.broadcasted_iota(jnp.int32, (BODY, TILE), 1) <= lax.rem(
        lax.broadcasted_iota(jnp.int32, (BODY, TILE), 0), TILE
    )
    bodies = [(g, b) for g in range(2) for b in range(ROWS // BODY)]

    def local_scores(t, g, b):
        q = q_v[t * 2 + g, b * BODY : (b + 1) * BODY, :]
        return dot_t(q, kvl[0 : (t + 1) * TILE, g * HEAD : (g + 1) * HEAD])

    def local_finish(t, g, b, s):
        rows = slice(b * BODY, (b + 1) * BODY)
        last = jnp.where(diag, s[:, t * TILE :], LOW)
        s = last if t == 0 else jnp.concatenate([s[:, : t * TILE], last], axis=1)
        top = jnp.max(s, axis=1, keepdims=True)
        p = jnp.exp2(s - top).astype(BF16)
        ol[t * 2 + g, rows, :] = dot(p, vl_aug[g, 0 : (t + 1) * TILE, :])
        ml[t * 2 + g, rows, :] = jnp.broadcast_to(top, (BODY, HEAD))

    def local_tile(t):
        s = local_scores(t, *bodies[0])
        for k, (g, b) in enumerate(bodies):
            ahead = local_scores(t, *bodies[k + 1]) if k + 1 < len(bodies) else None
            local_finish(t, g, b, s)
            s = ahead

    local_tile(1)
    local_tile(2)
    relay(0, 1, False)
    relay(1, 1, False)
    local_tile(3)

    got, eight = pl.ds(0, 6 * PIECE), pl.ds(0, 8 * PIECE)

    def anchor_here(ch):
        @pl.when(core == 1)
        def _():
            pltpu.make_async_copy(kva.at[got], kva.at[got], rest_recv.at[ch]).wait()

        @pl.when(core == 0)
        def _():
            pltpu.make_async_copy(kva.at[eight], kva.at[eight], rest_recv.at[ch]).wait()

        rows = pl.ds(ch * CROWS, CROWS)
        for g in range(2):
            va_aug[g, rows, 0:HEAD] = kva[rows, 256 + g * HEAD : 256 + (g + 1) * HEAD]

    def ctx_copy(t, g):
        cols = pl.ds(g * 512, 512)
        return pltpu.make_async_remote_copy(
            src_ref=ctx.at[t, :, cols], dst_ref=ctx_sib.at[t, :, cols],
            send_sem=ctx_send.at[t, g], recv_sem=ctx_recv.at[t, g],
            device_id=sibling, device_id_type=MESH,
        )

    def x_copy(t, c):
        cols = pl.ds(c * 512, 512)
        return pltpu.make_async_remote_copy(
            src_ref=sbuf.at[t, :, cols], dst_ref=rbuf.at[t, :, cols],
            send_sem=x_send.at[t, c], recv_sem=x_recv.at[t, c],
            device_id=far, device_id_type=MESH,
        )

    has_anchor = blk > 0

    def early_scores(g, b):
        q = q_v[g, b * BODY : (b + 1) * BODY, :]
        cols = slice(g * HEAD, (g + 1) * HEAD)
        return dot_t(q, kva[0:CROWS, cols]), dot_t(q, kvl[0:TILE, cols])

    def early_finish(g, b, s):
        rows = slice(b * BODY, (b + 1) * BODY)
        s = jnp.concatenate(
            [jnp.where(has_anchor, s[0], LOW), jnp.where(diag, s[1], LOW)], axis=1
        )
        top = jnp.max(s, axis=1, keepdims=True)
        p = jnp.exp2(s - top).astype(BF16)
        ol[g, rows, :] = dot(p[:, 0:CROWS], va_aug[g, 0:CROWS, :]) + dot(
            p[:, CROWS:], vl_aug[g, 0:TILE, :]
        )
        ml[g, rows, :] = jnp.broadcast_to(top, (BODY, HEAD))

    anchor_here(0)
    s = early_scores(*bodies[0])
    for k, (g, b) in enumerate(bodies):
        ahead = early_scores(*bodies[k + 1]) if k + 1 < len(bodies) else None
        early_finish(g, b, s)
        s = ahead
    anchor_here(1)

    def anchor_scores(t, g, b):
        q = q_v[t * 2 + g, b * BODY : (b + 1) * BODY, :]
        return dot_t(q, kva[0 if t else CROWS : ROWS, g * HEAD : (g + 1) * HEAD])

    def anchor_finish(t, g, b, s):
        rows = slice(b * BODY, (b + 1) * BODY)
        before = ml[t * 2 + g, rows, :][:, 0:1]
        both = jnp.maximum(jnp.max(s, axis=1, keepdims=True), before)
        top = jnp.where(has_anchor, both, before)
        p = jnp.exp2(s - jnp.where(has_anchor, both, -LOW)).astype(BF16)
        o = dot(p, va_aug[g, 0 if t else CROWS : ROWS, :]) + ol[t * 2 + g, rows, :] * jnp.exp2(before - top)
        res = (o[:, 0:HEAD] / o[:, HEAD:]).astype(BF16)
        for j in range(BODY // TILE):
            col = (g * 4 + b * (BODY // TILE) + j) * HEAD
            ctx[t, :, col : col + HEAD] = res[j * TILE : (j + 1) * TILE]

    def anchor_tile(t):
        s = anchor_scores(t, *bodies[0])
        for k, (g, b) in enumerate(bodies):
            ahead = anchor_scores(t, *bodies[k + 1]) if k + 1 < len(bodies) else None
            anchor_finish(t, g, b, s)
            s = ahead
            if b == ROWS // BODY - 1:
                ctx_copy(t, g).start()

    def near_part(t):
        acc_l[t] = dot(ctx[t], wo_a[1]) + dot(ctx_sib[t], wo_b[1])

    def sibling_here(t):
        for g in range(2):
            ctx_copy(t, g).wait_recv()

    anchor_tile(0)
    for cp in woa_cp:
        cp.wait()
    acc_r[...] = dot(ctx[0], wo_a[0])
    for cp in wob_cp:
        cp.wait_recv()
    sibling_here(0)
    for c in range(2):
        cols = slice(c * 512, (c + 1) * 512)
        sbuf[0, :, cols] = (acc_r[:, cols] + dot(ctx_sib[0], wo_b[0, :, cols])).astype(BF16)
        x_copy(0, c).start()
    for t in range(1, TILES):
        anchor_tile(t)
        near_part(t - 1)
        sibling_here(t)
        for c in range(2):
            cols = slice(c * 512, (c + 1) * 512)
            sbuf[t, :, cols] = (
                dot(ctx[t], wo_a[0, :, cols]) + dot(ctx_sib[t], wo_b[0, :, cols])
            ).astype(BF16)
            x_copy(t, c).start()
    near_part(TILES - 1)

    for t in range(TILES):
        for c in range(2):
            cols = slice(c * 512, (c + 1) * 512)
            x_copy(t, c).wait_recv()
            out[pl.ds(t * TILE, TILE), cols] = (
                acc_l[t, :, cols] + rbuf[t, :, cols].astype(F32)
            ).astype(BF16)

    for cp in wob_cp:
        cp.wait_send()
    for ch in range(CHUNKS):
        @pl.when(blk == 0)
        def _(ch=ch):
            pltpu.make_async_copy(kvl.at[got], kvl.at[got], first_send.at[ch]).wait()

            @pl.when(core == 0)
            def _():
                for part in range(2):
                    aside(ch, part).wait_send()

        @pl.when(core == 1)
        def _(ch=ch):
            for part in range(2):
                @pl.when(lines[1 - part] == 0)
                def _(part=part):
                    three = pl.ds(0, 3 * PIECE)
                    for grp in range(2):
                        pltpu.make_async_copy(
                            kva.at[three], kva.at[three], ring_send.at[ch, part, grp]
                        ).wait()

                        @pl.when(xl == 0)
                        def _(grp=grp):
                            forward(ch, part, grp).wait_send()

                home(ch, part).wait_send()
            for grp in range(2):
                pltpu.make_async_copy(kva.at[got], kva.at[got], rest_send.at[ch, grp]).wait()

    for t in range(TILES):
        for g in range(2):
            ctx_copy(t, g).wait_send()
            x_copy(t, g).wait_send()


def local(hidden_states, w_query, key_matrix, value_matrix, w_out):
    coarse_tab, fine_tab = rotary_tables(32)
    any_spec = pl.BlockSpec(memory_space=pl.ANY)
    dma = pltpu.SemaphoreType.DMA
    return pl.pallas_call(
        kernel,
        out_shape=pltpu.VMEM((ROWS, 1024), BF16),
        in_specs=[any_spec] * 7,
        out_specs=pl.BlockSpec(memory_space=pltpu.VMEM),
        scratch_shapes=[
            pltpu.VMEM((ROWS, WIDTH), BF16),
            pltpu.VMEM((2, WIDTH, 512), BF16),
            pltpu.VMEM((WIDTH, 512), BF16),
            pltpu.VMEM((2, 1024, 1024), BF16),
            pltpu.VMEM((2, 1024, 1024), BF16),
            pltpu.VMEM((2, ROWS // 16, HEAD), F32),
            pltpu.VMEM((2, 16, HEAD), F32),
            pltpu.VMEM((ROWS, HEAD), F32),
            pltpu.VMEM((ROWS, HEAD), F32),
            pltpu.VMEM((CROWS, 512), F32),
            pltpu.VMEM((ROWS, 512), BF16),
            pltpu.VMEM((ROWS, 512), BF16),
            pltpu.VMEM((ROWS, 512), BF16),
            pltpu.VMEM((TILES * 2, 4 * TILE, HEAD), BF16),
            pltpu.VMEM((2, ROWS, 2 * HEAD), BF16),
            pltpu.VMEM((2, ROWS, 2 * HEAD), BF16),
            pltpu.VMEM((TILES * 2, 4 * TILE, 2 * HEAD), F32),
            pltpu.VMEM((TILES * 2, 4 * TILE, HEAD), F32),
            pltpu.VMEM((TILES, TILE, 1024), BF16),
            pltpu.VMEM((TILES, TILE, 1024), BF16),
            pltpu.VMEM((TILE, 1024), F32),
            pltpu.VMEM((TILES, TILE, 1024), F32),
            pltpu.VMEM((TILES, TILE, 1024), BF16),
            pltpu.VMEM((TILES, TILE, 1024), BF16),
            dma((3,)), dma((2, 2)), dma((2,)), dma((2,)), dma((2,)), dma((2,)), dma((2,)),
            dma((CHUNKS,)), dma((CHUNKS, 2)), dma((CHUNKS, 2, 2)), dma((CHUNKS, 2, 2)),
            dma((CHUNKS, 2, 2)), dma((CHUNKS, 2)), dma((CHUNKS, 2)), dma((CHUNKS,)),
            dma((TILES, 2)), dma((TILES, 2)), dma((TILES, 2)), dma((TILES, 2)),
            dma((CHUNKS, 2)),
        ],
        compiler_params=pltpu.CompilerParams(
            collective_id=0, has_side_effects=True, vmem_limit_bytes=60 * 2**20
        ),
        name="layer",
    )(
        hidden_states, w_query, key_matrix, value_matrix, w_out,
        jnp.asarray(coarse_tab), jnp.asarray(fine_tab),
    )


def solution(mesh):
    in_specs = (P("blk", None), P(None, "head"), P(None, "head"), P(None, "head"), P("head", None))
    out_specs = P("blk", "head")
    return jax.shard_map(local, mesh=mesh, in_specs=in_specs, out_specs=out_specs, check_vma=False)
```

```python
import jax
import jax.numpy as jnp
import numpy as np
from jax import lax
from jax.experimental import pallas as pl
from jax.experimental.pallas import tpu as pltpu
from jax.sharding import PartitionSpec as P

HEAD = 128
ROWS = 512
WIDTH = 4096
PART = 64
PARTS = ROWS // PART
TILES = ((0, 128), (128, 128), (256, 128), (384, 128))
KROWS = 256
CHUNKS = 2
CROWS = ROWS // CHUNKS
PIECE = CROWS // 8
EARLY = ROWS - CROWS
BODY = 4 * PART
ROOT, PLACE, REST = range(3)
PLAN = {
    0: ((ROOT, 0, 0),),
    1: ((ROOT, 1, 0), (REST, 0, 0)),
    2: ((ROOT, 0, 1), (ROOT, 1, 1), (REST, 0, 1)),
    3: ((PLACE, 0, 0), (PLACE, 1, 0)),
    4: ((PLACE, 0, 1), (PLACE, 1, 1)),
}
MESH = pl.DeviceIdType.MESH
LOW = -1e30
F32 = jnp.float32
BF16 = jnp.bfloat16


def rotary_tables(blocks):
    freqs = 500000.0 ** (-2.0 * np.arange(HEAD // 2) / HEAD)

    def table(tokens):
        angle = tokens[..., None] * freqs
        both = [np.concatenate([f(angle)] * 2, axis=-1) for f in (np.cos, np.sin)]
        return np.stack(both, axis=-3).astype(np.float32)

    return table(np.arange(blocks * ROWS // 16).reshape(blocks, -1) * 16.0), table(np.arange(16.0))


def dot(a, b):
    return jnp.dot(a, b, preferred_element_type=F32)


def dot_t(a, b):
    return lax.dot_general(a, b, (((1,), (1,)), ((), ())), preferred_element_type=F32)


def kernel(
    hid, wq, wk, wv, wo, coarse_tab, fine_tab, out,
    hid_v, wq_v, wkv_v, wo_a, wo_b, coarse, fine, cos_v, sin_v,
    kv_acc, kvl, kva, stage, q_v, vl_aug, va_aug, ol, ml, ctx, ctx_sib, acc_r, acc_l, sbuf, rbuf,
    hid_sem, wkv_sem, tab_sem, wq_sem, woa_sem, wob_send, wob_recv,
    first_send, aside_send, mine_recv, ring_send, fwd_send, rest_send, home_send, rest_recv,
    ctx_send, ctx_recv, x_send, x_recv, own_sem,
):
    blk = lax.axis_index("blk")
    head = lax.axis_index("head")
    xl = lax.rem(blk, 2)
    pos = blk // 2
    y, z = pos // 4, lax.rem(pos, 4)
    xh, core = head // 2, lax.rem(head, 2)

    def along(part, d):
        if part == 0:
            return (lax.rem(y + d, 4) * 4 + z) * 2 + xl
        return (y * 4 + lax.rem(z + d, 4)) * 2 + xl

    rings = [[along(part, d) for d in (1, 2, 3)] for part in range(2)]
    xl_peer = pos * 2 + 1 - xl
    zero, one = xh * 2, xh * 2 + 1
    sibling = (blk, xh * 2 + 1 - core)
    far_head = (1 - xh) * 2 + core
    far = (blk, far_head)

    barrier = pltpu.get_barrier_semaphore()
    friends = [(b, h) for b in rings[0] + rings[1] for h in (zero, one)]
    friends += [(xl_peer, head), sibling, far]
    for friend in friends:
        pl.semaphore_signal(barrier, inc=1, device_id=friend, device_id_type=MESH)

    hid_cp = [
        pltpu.make_async_copy(
            hid.at[pl.ds(0, KROWS), pl.ds(d * 2048, 2048)],
            hid_v.at[pl.ds(0, KROWS), pl.ds(d * 2048, 2048)],
            hid_sem.at[d],
        )
        for d in range(2)
    ]
    later_cp = pltpu.make_async_copy(
        hid.at[pl.ds(KROWS, KROWS)], hid_v.at[pl.ds(KROWS, KROWS)], hid_sem.at[2]
    )
    half = WIDTH // 2
    wkv_cp = [
        pltpu.make_async_copy(
            w.at[pl.ds(d * half, half)],
            wkv_v.at[pl.ds(d * half, half), pl.ds(i * 256, 256)],
            wkv_sem.at[d, i],
        )
        for d in range(2)
        for i, w in enumerate((wk, wv))
    ]
    tab_cp = [
        pltpu.make_async_copy(coarse_tab.at[blk], coarse, tab_sem.at[0]),
        pltpu.make_async_copy(fine_tab, fine, tab_sem.at[1]),
    ]
    wq_cp = [
        pltpu.make_async_copy(wq.at[:, pl.ds(n * 512, 512)], wq_v.at[n], wq_sem.at[n])
        for n in range(2)
    ]
    woa_cp = [
        pltpu.make_async_copy(
            wo.at[:, pl.ds(pl.multiple_of(h * 1024, 1024), 1024)], wo_a.at[i], woa_sem.at[i]
        )
        for i, h in enumerate((far_head, head))
    ]
    first_half = [hid_cp[0], wkv_cp[0], wkv_cp[1]]
    second_half = [hid_cp[1], wkv_cp[2], wkv_cp[3]]
    for cp in tab_cp + first_half + second_half + [later_cp]:
        cp.start()
    def make_tables():
        lane = lax.broadcasted_iota(jnp.int32, (16, HEAD), 1)
        sign = jnp.where(lane < HEAD // 2, -1.0, 1.0)
        cf, sf = fine[0], fine[1]

        def step(i, carry):
            ca, sa = coarse[0, pl.ds(i, 1), :], coarse[1, pl.ds(i, 1), :]
            rows = pl.ds(pl.multiple_of(i * 16, 16), 16)
            cos_v[rows, :] = ca * cf - sa * sf
            sin_v[rows, :] = (sa * cf + ca * sf) * sign
            return carry

        lax.fori_loop(0, ROWS // 16, step, 0, unroll=4)

    scale = float(1 / np.sqrt(HEAD))

    def turn(x, c, s):
        return x * c + pltpu.roll(x, HEAD // 2, 1) * s

    lines = (y, z)
    held = (stage, kva)

    def piece(ch, part, j):
        return pl.ds(pl.multiple_of(ch * CROWS + (part * 4 + j) * PIECE, PIECE), PIECE)

    def push(src, dst, ch, part, j, send_sem, recv_sem, target):
        rows = piece(ch, part, j)
        return pltpu.make_async_remote_copy(
            src_ref=src.at[rows], dst_ref=dst.at[rows], send_sem=send_sem, recv_sem=recv_sem,
            device_id=target, device_id_type=MESH,
        )

    def own_copy(ch, part):
        rows = piece(ch, part, 0)
        return pltpu.make_async_copy(kvl.at[rows], kva.at[rows], own_sem.at[ch, part])

    def aside(ch, part):
        return push(
            kvl, stage, ch, part, 0, aside_send.at[ch, part], mine_recv.at[ch, part, 0], sibling
        )

    def first(ch, part, d, grp):
        return push(
            kvl, held[grp], ch, part, d, first_send.at[ch], mine_recv.at[ch, part, grp],
            (rings[part][d - 1], one),
        )

    def forward(ch, part, grp):
        return push(
            held[grp], held[grp], ch, part, lines[part], fwd_send.at[ch, part, grp],
            mine_recv.at[ch, part, grp], (xl_peer, one),
        )

    def across(ch, part, d, grp):
        return push(
            held[grp], held[grp], ch, part, lines[part], ring_send.at[ch, part, grp],
            mine_recv.at[ch, part, grp], (rings[1 - part][d - 1], one),
        )

    def rest(ch, part, d, grp):
        return push(
            held[grp], kva, ch, part, lines[part], rest_send.at[ch, grp], rest_recv.at[ch],
            (rings[part][d - 1], (zero, one)[grp]),
        )

    def home(ch, part):
        return push(
            stage, kva, ch, part, lines[part], home_send.at[ch, part], rest_recv.at[ch], sibling
        )

    def scatter_chunk(ch):
        for grp in range(2):
            @pl.when(jnp.logical_and(blk == 0, core == grp))
            def _(grp=grp):
                for part in range(2):
                    for d in (1, 2, 3):
                        first(ch, part, d, grp).start()
                for part in range(2):
                    if grp == 0:
                        aside(ch, part).start()
                    else:
                        own_copy(ch, part).start()

    def relay_part(ch, part, early):
        at_root = lines[1 - part] == 0

        @pl.when(at_root if early else jnp.logical_not(at_root))
        def _():
            forward(ch, part, 0).wait_recv()
            if early:
                @pl.when(blk == 0)
                def _():
                    own_copy(ch, part).wait()

                @pl.when(blk != 0)
                def _():
                    forward(ch, part, 1).wait_recv()
            else:
                forward(ch, part, 1).wait_recv()
            if early:
                for grp in range(2):
                    @pl.when(xl == 0)
                    def _(grp=grp):
                        forward(ch, part, grp).start()

                    for d in (1, 2, 3):
                        across(ch, part, d, grp).start()
            else:
                send_rest(ch, part)

    def send_rest(ch, part):
        for grp in range(2):
            for d in (1, 2, 3):
                rest(ch, part, d, grp).start()
        home(ch, part).start()

    def root_rest(side):
        for part in range(2):
            mine = jnp.logical_and(lines[1 - part] == 0, xl == side)

            @pl.when(jnp.logical_and(mine, core == 1))
            def _(part=part):
                for ch in range(CHUNKS):
                    send_rest(ch, part)

    def relay(early, ch, side):
        @pl.when(jnp.logical_and(xl == side, core == 1))
        def _():
            for part in range(2):
                relay_part(ch, part, early)

    def slot(k):
        for what, ch, side in PLAN.get(k, ()):
            if what == REST:
                root_rest(side)
            else:
                relay(what == ROOT, ch, side)

    for cp in first_half:
        cp.wait()
    for i in range(ROWS // KROWS):
        rows = pl.ds(i * KROWS, KROWS)
        if i == 0:
            kv_acc[...] = dot(hid_v[rows, 0:half], wkv_v[0:half, :])
            for cp in second_half:
                cp.wait()
            for cp in wq_cp:
                cp.start()
            kv_acc[...] += dot(hid_v[rows, half:], wkv_v[half:, :])
            for cp in tab_cp:
                cp.wait()
            make_tables()
            kv = kv_acc[...]
        else:
            later_cp.wait()
            kv = dot(hid_v[rows, :], wkv_v[...])
        c, s = cos_v[rows, :], sin_v[rows, :]
        for g in range(2):
            cols = slice(g * HEAD, (g + 1) * HEAD)
            kvl[rows, cols] = turn(kv[:, cols], c, s).astype(BF16)
        kvl[rows, 256:512] = kv[:, 256:512].astype(BF16)
    pl.semaphore_wait(barrier, len(friends))
    for ch in range(CHUNKS):
        scatter_chunk(ch)
    for g in range(2):
        vl_aug[g, :, 0:HEAD] = kvl[:, 256 + g * HEAD : 256 + (g + 1) * HEAD]
        vl_aug[g, :, HEAD:] = jnp.ones((ROWS, HEAD), BF16)
        va_aug[g, :, HEAD:] = jnp.ones((ROWS, HEAD), BF16)

    other = 1 - core
    wob_cp = [
        pltpu.make_async_remote_copy(
            src_ref=wo.at[:, pl.ds(pl.multiple_of(h * 1024, 1024), 1024)], dst_ref=wo_b.at[i],
            send_sem=wob_send.at[i], recv_sem=wob_recv.at[i],
            device_id=sibling, device_id_type=MESH,
        )
        for i, h in enumerate(((1 - xh) * 2 + other, xh * 2 + other))
    ]
    for cp in woa_cp + wob_cp:
        cp.start()

    slot(0)
    for n in range(4):
        g, m = n // 2, n % 2
        if m == 0:
            wq_cp[g].wait()
        x = dot(hid_v[m * 256 : (m + 1) * 256, :], wq_v[g])
        rows = slice(m * 256, (m + 1) * 256)
        c, s = cos_v[rows, :] * scale, sin_v[rows, :] * scale
        for j in range(4):
            turned = turn(x[:, j * HEAD : (j + 1) * HEAD], c, s).astype(BF16)
            for k in range(4):
                q_v[(4 * m + k) * 2 + g, j * PART : (j + 1) * PART, :] = turned[
                    k * PART : (k + 1) * PART
                ]
        slot(n + 1)

    row = lax.rem(lax.broadcasted_iota(jnp.int32, (BODY, HEAD), 0), PART)
    col = lax.broadcasted_iota(jnp.int32, (BODY, HEAD), 1)
    diag = (col <= row, col <= row + PART)

    def in_turn(bodies, scores, finish):
        every = [scores(*body) for body in bodies]
        for body, s in zip(bodies, every):
            finish(*body, s)

    def bodies_of(t):
        start, size = TILES[t]
        return [(b, g) for g in range(2) for b in range(start // PART, (start + size) // PART)]

    def local_scores(b, g):
        keys = (b // 2 + 1) * HEAD
        return dot_t(q_v[b * 2 + g], kvl[0:keys, g * HEAD : (g + 1) * HEAD])

    def local_finish(b, g, s):
        before = b // 2 * HEAD
        last = jnp.where(diag[b % 2], s[:, before:], LOW)
        s = jnp.concatenate([s[:, :before], last], axis=1) if before else last
        top = jnp.max(s, axis=1, keepdims=True)
        p = jnp.exp(s - top).astype(BF16)
        ol[b * 2 + g] = dot(p, vl_aug[g, 0 : before + HEAD, :])
        ml[b * 2 + g] = jnp.broadcast_to(top, (BODY, HEAD))

    for t in range(1, len(TILES)):
        in_turn(bodies_of(t), local_scores, local_finish)
        slot(4 + t)

    got, eight = pl.ds(0, 6 * PIECE), pl.ds(0, 8 * PIECE)

    def anchor_here(ch):
        @pl.when(core == 1)
        def _():
            pltpu.make_async_copy(kva.at[got], kva.at[got], rest_recv.at[ch]).wait()

        @pl.when(core == 0)
        def _():
            pltpu.make_async_copy(kva.at[eight], kva.at[eight], rest_recv.at[ch]).wait()

        rows = pl.ds(ch * CROWS, CROWS)
        for g in range(2):
            va_aug[g, rows, 0:HEAD] = kva[rows, 256 + g * HEAD : 256 + (g + 1) * HEAD]

    def tile_rows(t):
        return pl.ds(*TILES[t])

    def ctx_copy(t, g):
        cols = pl.ds(g * 512, 512)
        return pltpu.make_async_remote_copy(
            src_ref=ctx.at[tile_rows(t), cols], dst_ref=ctx_sib.at[tile_rows(t), cols],
            send_sem=ctx_send.at[t, g], recv_sem=ctx_recv.at[t, g],
            device_id=sibling, device_id_type=MESH,
        )

    def x_copy(t, c):
        cols = pl.ds(c * 512, 512)
        return pltpu.make_async_remote_copy(
            src_ref=sbuf.at[tile_rows(t), cols], dst_ref=rbuf.at[tile_rows(t), cols],
            send_sem=x_send.at[t, c], recv_sem=x_recv.at[t, c],
            device_id=far, device_id_type=MESH,
        )

    has_anchor = blk > 0

    def early_scores(b, g):
        q, cols = q_v[b * 2 + g], slice(g * HEAD, (g + 1) * HEAD)
        return dot_t(q, kva[0:EARLY, cols]), dot_t(q, kvl[0:HEAD, cols])

    def early_finish(b, g, s):
        s = jnp.concatenate(
            [jnp.where(has_anchor, s[0], LOW), jnp.where(diag[b % 2], s[1], LOW)], axis=1
        )
        top = jnp.max(s, axis=1, keepdims=True)
        p = jnp.exp(s - top).astype(BF16)
        ol[b * 2 + g] = dot(p[:, 0:EARLY], va_aug[g, 0:EARLY, :]) + dot(
            p[:, EARLY:], vl_aug[g, 0:HEAD, :]
        )
        ml[b * 2 + g] = jnp.broadcast_to(top, (BODY, HEAD))

    for ch in range(CHUNKS - 1):
        anchor_here(ch)
    in_turn(bodies_of(0), early_scores, early_finish)
    anchor_here(CHUNKS - 1)

    def first_key(b):
        return 0 if b * PART >= TILES[0][1] else EARLY

    def anchor_scores(b, g):
        return dot_t(q_v[b * 2 + g], kva[first_key(b) :, g * HEAD : (g + 1) * HEAD])

    def anchor_finish(b, g, s):
        before = ml[b * 2 + g][:, 0:1]
        both = jnp.maximum(jnp.max(s, axis=1, keepdims=True), before)
        top = jnp.where(has_anchor, both, before)
        p = jnp.exp(s - jnp.where(has_anchor, both, -LOW)).astype(BF16)
        o = dot(p, va_aug[g, first_key(b) :, :]) + ol[b * 2 + g] * jnp.exp(before - top)
        res = (o[:, 0:HEAD] / o[:, HEAD:]).astype(BF16)
        for j in range(4):
            cols = slice((g * 4 + j) * HEAD, (g * 4 + j + 1) * HEAD)
            ctx[b * PART : (b + 1) * PART, cols] = res[j * PART : (j + 1) * PART]

    def anchor_tile(t):
        ends = TILES[t][0] + TILES[t][1] - PART

        def finish(b, g, s):
            anchor_finish(b, g, s)
            if b * PART == ends:
                ctx_copy(t, g).start()

        in_turn(bodies_of(t), anchor_scores, finish)

    def near_part(start):
        rows = pl.ds(start, 256)
        acc_l[rows, :] = dot(ctx[rows, :], wo_a[1]) + dot(ctx_sib[rows, :], wo_b[1])

    def sibling_here(t):
        for g in range(2):
            ctx_copy(t, g).wait_recv()

    anchor_tile(0)
    for cp in woa_cp:
        cp.wait()
    head_rows = tile_rows(0)
    acc_r[...] = dot(ctx[head_rows, :], wo_a[0])
    for cp in wob_cp:
        cp.wait_recv()
    sibling_here(0)
    for c in range(2):
        cols = slice(c * 512, (c + 1) * 512)
        sbuf[head_rows, cols] = (
            acc_r[:, cols] + dot(ctx_sib[head_rows, :], wo_b[0, :, cols])
        ).astype(BF16)
        x_copy(0, c).start()
    def far_part(t):
        sibling_here(t)
        rows = tile_rows(t)
        for c in range(2):
            cols = slice(c * 512, (c + 1) * 512)
            sbuf[rows, cols] = (
                dot(ctx[rows, :], wo_a[0, :, cols]) + dot(ctx_sib[rows, :], wo_b[0, :, cols])
            ).astype(BF16)
            x_copy(t, c).start()

    for t in range(1, len(TILES)):
        anchor_tile(t)
        if t > 1:
            far_part(t - 1)
    far_part(len(TILES) - 1)
    for start in range(0, ROWS, 256):
        near_part(start)

    for t in range(len(TILES)):
        rows = tile_rows(t)
        for c in range(2):
            cols = slice(c * 512, (c + 1) * 512)
            x_copy(t, c).wait_recv()
            out[rows, cols] = (acc_l[rows, cols] + rbuf[rows, cols].astype(F32)).astype(BF16)

    for cp in wob_cp:
        cp.wait_send()
    for ch in range(CHUNKS):
        @pl.when(blk == 0)
        def _(ch=ch):
            pltpu.make_async_copy(kvl.at[got], kvl.at[got], first_send.at[ch]).wait()

            @pl.when(core == 0)
            def _():
                for part in range(2):
                    aside(ch, part).wait_send()

        @pl.when(core == 1)
        def _(ch=ch):
            for part in range(2):
                @pl.when(lines[1 - part] == 0)
                def _(part=part):
                    three = pl.ds(0, 3 * PIECE)
                    for grp in range(2):
                        pltpu.make_async_copy(
                            kva.at[three], kva.at[three], ring_send.at[ch, part, grp]
                        ).wait()

                        @pl.when(xl == 0)
                        def _(grp=grp):
                            forward(ch, part, grp).wait_send()

                home(ch, part).wait_send()
            for grp in range(2):
                pltpu.make_async_copy(kva.at[got], kva.at[got], rest_send.at[ch, grp]).wait()

    for t in range(len(TILES)):
        for g in range(2):
            ctx_copy(t, g).wait_send()
            x_copy(t, g).wait_send()


def local(hidden_states, w_query, key_matrix, value_matrix, w_out):
    coarse_tab, fine_tab = rotary_tables(32)
    any_spec = pl.BlockSpec(memory_space=pl.ANY)
    dma = pltpu.SemaphoreType.DMA
    return pl.pallas_call(
        kernel,
        out_shape=pltpu.VMEM((ROWS, 1024), BF16),
        in_specs=[any_spec] * 7,
        out_specs=pl.BlockSpec(memory_space=pltpu.VMEM),
        scratch_shapes=[
            pltpu.VMEM((ROWS, WIDTH), BF16),
            pltpu.VMEM((2, WIDTH, 512), BF16),
            pltpu.VMEM((WIDTH, 512), BF16),
            pltpu.VMEM((2, 1024, 1024), BF16),
            pltpu.VMEM((2, 1024, 1024), BF16),
            pltpu.VMEM((2, ROWS // 16, HEAD), F32),
            pltpu.VMEM((2, 16, HEAD), F32),
            pltpu.VMEM((ROWS, HEAD), F32),
            pltpu.VMEM((ROWS, HEAD), F32),
            pltpu.VMEM((KROWS, 512), F32),
            pltpu.VMEM((ROWS, 512), BF16),
            pltpu.VMEM((ROWS, 512), BF16),
            pltpu.VMEM((ROWS, 512), BF16),
            pltpu.VMEM((PARTS * 2, BODY, HEAD), BF16),
            pltpu.VMEM((2, ROWS, 2 * HEAD), BF16),
            pltpu.VMEM((2, ROWS, 2 * HEAD), BF16),
            pltpu.VMEM((PARTS * 2, BODY, 2 * HEAD), F32),
            pltpu.VMEM((PARTS * 2, BODY, HEAD), F32),
            pltpu.VMEM((ROWS, 1024), BF16),
            pltpu.VMEM((ROWS, 1024), BF16),
            pltpu.VMEM((TILES[0][1], 1024), F32),
            pltpu.VMEM((ROWS, 1024), F32),
            pltpu.VMEM((ROWS, 1024), BF16),
            pltpu.VMEM((ROWS, 1024), BF16),
            dma((3,)), dma((2, 2)), dma((2,)), dma((2,)), dma((2,)), dma((2,)), dma((2,)),
            dma((CHUNKS,)), dma((CHUNKS, 2)), dma((CHUNKS, 2, 2)), dma((CHUNKS, 2, 2)),
            dma((CHUNKS, 2, 2)), dma((CHUNKS, 2)), dma((CHUNKS, 2)), dma((CHUNKS,)),
            dma((len(TILES), 2)), dma((len(TILES), 2)),
            dma((len(TILES), 2)), dma((len(TILES), 2)),
            dma((CHUNKS, 2)),
        ],
        compiler_params=pltpu.CompilerParams(
            collective_id=0, has_side_effects=True, vmem_limit_bytes=60 * 2**20
        ),
        name="layer",
    )(
        hidden_states, w_query, key_matrix, value_matrix, w_out,
        jnp.asarray(coarse_tab), jnp.asarray(fine_tab),
    )


def solution(mesh):
    in_specs = (P("blk", None), P(None, "head"), P(None, "head"), P(None, "head"), P("head", None))
    out_specs = P("blk", "head")
    return jax.shard_map(local, mesh=mesh, in_specs=in_specs, out_specs=out_specs, check_vma=False)
```

```python
import jax
import jax.numpy as jnp
import numpy as np
from jax import lax
from jax.experimental import pallas as pl
from jax.experimental.pallas import tpu as pltpu
from jax.sharding import PartitionSpec as P

HEAD = 128
ROWS = 512
WIDTH = 4096
PART = 64
PARTS = ROWS // PART
TILES = ((0, 128), (128, 128), (256, 128), (384, 128))
KROWS = 256
CHUNKS = 2
CROWS = ROWS // CHUNKS
PIECE = CROWS // 8
EARLY = ROWS - CROWS
BODY = 4 * PART
ROOT, PLACE, REST = range(3)
PLAN = {
    0: ((ROOT, 0, 0),),
    1: ((ROOT, 1, 0), (REST, 0, 0)),
    2: ((ROOT, 0, 1), (ROOT, 1, 1), (REST, 0, 1)),
    3: ((PLACE, 0, 0), (PLACE, 1, 0)),
    4: ((PLACE, 0, 1), (PLACE, 1, 1)),
}
MESH = pl.DeviceIdType.MESH
LOW = -1e30
F32 = jnp.float32
BF16 = jnp.bfloat16


def rotary_tables(blocks):
    freqs = 500000.0 ** (-2.0 * np.arange(HEAD // 2) / HEAD)

    def table(tokens):
        angle = tokens[..., None] * freqs
        both = [np.concatenate([f(angle)] * 2, axis=-1) for f in (np.cos, np.sin)]
        return np.stack(both, axis=-3).astype(np.float32)

    return table(np.arange(blocks * ROWS // 16).reshape(blocks, -1) * 16.0), table(np.arange(16.0))


def dot(a, b):
    return jnp.dot(a, b, preferred_element_type=F32)


def dot_t(a, b):
    return lax.dot_general(a, b, (((1,), (1,)), ((), ())), preferred_element_type=F32)


def kernel(
    hid, wq, wk, wv, wo, coarse_tab, fine_tab, out,
    hid_v, wq_v, wkv_v, wo_a, wo_b, coarse, fine, cos_v, sin_v,
    kv_acc, kvl, kva, stage, q_v, vl_aug, va_aug, ol, ml, ctx, ctx_sib, acc_r, acc_l, sbuf, rbuf,
    load_sem, wob_send, wob_recv, first_send, mine_recv, ring_send, rest_send, rest_recv,
    ctx_send, ctx_recv, x_send, x_recv,
):
    blk = lax.axis_index("blk")
    head = lax.axis_index("head")
    xl = lax.rem(blk, 2)
    pos = blk // 2
    y, z = pos // 4, lax.rem(pos, 4)
    xh, core = head // 2, lax.rem(head, 2)

    def along(part, d):
        if part == 0:
            return (lax.rem(y + d, 4) * 4 + z) * 2 + xl
        return (y * 4 + lax.rem(z + d, 4)) * 2 + xl

    rings = [[along(part, d) for d in (1, 2, 3)] for part in range(2)]
    xl_peer = pos * 2 + 1 - xl
    zero, one = xh * 2, xh * 2 + 1
    sibling = (blk, xh * 2 + 1 - core)
    far_head = (1 - xh) * 2 + core
    far = (blk, far_head)

    barrier = pltpu.get_barrier_semaphore()
    friends = [(b, h) for b in rings[0] + rings[1] for h in (zero, one)]
    friends += [(xl_peer, head), sibling, far]
    for friend in friends:
        pl.semaphore_signal(barrier, inc=1, device_id=friend, device_id_type=MESH)

    hid_cp = [
        pltpu.make_async_copy(
            hid.at[pl.ds(0, KROWS), pl.ds(d * 2048, 2048)],
            hid_v.at[pl.ds(0, KROWS), pl.ds(d * 2048, 2048)],
            load_sem.at[d],
        )
        for d in range(2)
    ]
    later_cp = pltpu.make_async_copy(
        hid.at[pl.ds(KROWS, KROWS)], hid_v.at[pl.ds(KROWS, KROWS)], load_sem.at[2]
    )
    half = WIDTH // 2
    wkv_cp = [
        pltpu.make_async_copy(
            w.at[pl.ds(d * half, half)],
            wkv_v.at[pl.ds(d * half, half), pl.ds(i * 256, 256)],
            load_sem.at[d],
        )
        for d in range(2)
        for i, w in enumerate((wk, wv))
    ]
    tab_cp = [
        pltpu.make_async_copy(coarse_tab.at[blk], coarse, load_sem.at[3]),
        pltpu.make_async_copy(fine_tab, fine, load_sem.at[3]),
    ]
    wq_cp = [
        pltpu.make_async_copy(wq.at[:, pl.ds(n * 512, 512)], wq_v.at[n], load_sem.at[n])
        for n in range(2)
    ]
    woa_cp = [
        pltpu.make_async_copy(
            wo.at[:, pl.ds(pl.multiple_of(h * 1024, 1024), 1024)], wo_a.at[i], load_sem.at[2]
        )
        for i, h in enumerate((far_head, head))
    ]

    def wait_all(like, sem):
        pltpu.make_async_copy(like, like, sem).wait()

    first_half = [hid_cp[0], wkv_cp[0], wkv_cp[1]]
    second_half = [hid_cp[1], wkv_cp[2], wkv_cp[3]]
    for cp in tab_cp + first_half + second_half + [later_cp]:
        cp.start()
    def make_tables():
        lane = lax.broadcasted_iota(jnp.int32, (16, HEAD), 1)
        sign = jnp.where(lane < HEAD // 2, -1.0, 1.0)
        cf, sf = fine[0], fine[1]

        def step(i, carry):
            ca, sa = coarse[0, pl.ds(i, 1), :], coarse[1, pl.ds(i, 1), :]
            rows = pl.ds(pl.multiple_of(i * 16, 16), 16)
            cos_v[rows, :] = ca * cf - sa * sf
            sin_v[rows, :] = (sa * cf + ca * sf) * sign
            return carry

        lax.fori_loop(0, ROWS // 16, step, 0, unroll=4)

    scale = float(1 / np.sqrt(HEAD))

    def turn(x, c, s):
        return x * c + pltpu.roll(x, HEAD // 2, 1) * s

    lines = (y, z)
    held = (stage, kva)

    def piece(ch, part, j):
        return pl.ds(pl.multiple_of(ch * CROWS + (part * 4 + j) * PIECE, PIECE), PIECE)

    def push(src, dst, ch, part, j, send_sem, recv_sem, target):
        rows = piece(ch, part, j)
        return pltpu.make_async_remote_copy(
            src_ref=src.at[rows], dst_ref=dst.at[rows], send_sem=send_sem, recv_sem=recv_sem,
            device_id=target, device_id_type=MESH,
        )

    def aside(ch, part):
        return push(
            kvl, stage, ch, part, 0, first_send, mine_recv.at[ch, part], sibling
        )

    def first(ch, part, d, grp):
        return push(
            kvl, held[grp], ch, part, d, first_send, mine_recv.at[ch, part],
            (rings[part][d - 1], one),
        )

    def forward(ch, part, grp):
        return push(
            held[grp], held[grp], ch, part, lines[part], ring_send.at[part],
            mine_recv.at[ch, part], (xl_peer, one),
        )

    def across(ch, part, d, grp):
        return push(
            held[grp], held[grp], ch, part, lines[part], ring_send.at[part],
            mine_recv.at[ch, part], (rings[1 - part][d - 1], one),
        )

    def rest(ch, part, d, grp):
        return push(
            held[grp], kva, ch, part, lines[part], rest_send, rest_recv.at[ch],
            (rings[part][d - 1], (zero, one)[grp]),
        )

    def home(ch, part):
        return push(
            stage, kva, ch, part, lines[part], rest_send, rest_recv.at[ch], sibling
        )

    def scatter_chunk(ch):
        for grp in range(2):
            @pl.when(jnp.logical_and(blk == 0, core == grp))
            def _(grp=grp):
                for part in range(2):
                    for d in (2, 1, 3):
                        first(ch, part, d, grp).start()
                for part in range(2):
                    if grp == 0:
                        aside(ch, part).start()
                    else:
                        start = ch * CROWS + part * 4 * PIECE
                        kva[start : start + PIECE, :] = kvl[start : start + PIECE, :]

    def relay_part(ch, part, early):
        at_root = lines[1 - part] == 0

        @pl.when(at_root if early else jnp.logical_not(at_root))
        def _():
            @pl.when(blk == 0)
            def _():
                wait_all(kva.at[pl.ds(0, PIECE)], mine_recv.at[ch, part])

            @pl.when(blk != 0)
            def _():
                wait_all(kva.at[pl.ds(0, 2 * PIECE)], mine_recv.at[ch, part])

            if early:
                for grp in range(2):
                    @pl.when(xl == 0)
                    def _(grp=grp):
                        forward(ch, part, grp).start()

                    for d in (2, 1, 3):
                        across(ch, part, d, grp).start()
            else:
                send_rest(ch, part)

    def send_rest(ch, part):
        for grp in range(2):
            for d in (2, 1, 3):
                rest(ch, part, d, grp).start()
        home(ch, part).start()

    def root_rest(side):
        for part in range(2):
            mine = jnp.logical_and(lines[1 - part] == 0, xl == side)

            @pl.when(jnp.logical_and(mine, core == 1))
            def _(part=part):
                for ch in range(CHUNKS):
                    send_rest(ch, part)

    def relay(early, ch, side):
        @pl.when(jnp.logical_and(xl == side, core == 1))
        def _():
            for part in range(2):
                relay_part(ch, part, early)

    def slot(k):
        for what, ch, side in PLAN.get(k, ()):
            if what == REST:
                root_rest(side)
            else:
                relay(what == ROOT, ch, side)

    wait_all(hid_v.at[pl.ds(0, 384)], load_sem.at[0])
    for i in range(ROWS // KROWS):
        rows = pl.ds(i * KROWS, KROWS)
        if i == 0:
            kv_acc[...] = dot(hid_v[rows, 0:half], wkv_v[0:half, :])
            wait_all(hid_v.at[pl.ds(0, 384)], load_sem.at[1])
            for cp in wq_cp:
                cp.start()
            kv_acc[...] += dot(hid_v[rows, half:], wkv_v[half:, :])
            wait_all(cos_v.at[pl.ds(0, 96)], load_sem.at[3])
            make_tables()
            kv = kv_acc[...]
        else:
            later_cp.wait()
            kv = dot(hid_v[rows, :], wkv_v[...])
        c, s = cos_v[rows, :], sin_v[rows, :]
        for g in range(2):
            cols = slice(g * HEAD, (g + 1) * HEAD)
            kvl[rows, cols] = turn(kv[:, cols], c, s).astype(BF16)
        kvl[rows, 256:512] = kv[:, 256:512].astype(BF16)
    pl.semaphore_wait(barrier, len(friends))
    for ch in range(CHUNKS):
        scatter_chunk(ch)
    for g in range(2):
        vl_aug[g, :, 0:HEAD] = kvl[:, 256 + g * HEAD : 256 + (g + 1) * HEAD]
        vl_aug[g, :, HEAD:] = jnp.ones((ROWS, HEAD), BF16)
        va_aug[g, :, HEAD:] = jnp.ones((ROWS, HEAD), BF16)

    other = 1 - core
    wob_cp = [
        pltpu.make_async_remote_copy(
            src_ref=wo.at[:, pl.ds(pl.multiple_of(h * 1024, 1024), 1024)], dst_ref=wo_b.at[i],
            send_sem=wob_send, recv_sem=wob_recv,
            device_id=sibling, device_id_type=MESH,
        )
        for i, h in enumerate(((1 - xh) * 2 + other, xh * 2 + other))
    ]
    for cp in woa_cp + wob_cp:
        cp.start()

    slot(0)
    for n in range(4):
        g, m = n // 2, n % 2
        if m == 0:
            wq_cp[g].wait()
        x = dot(hid_v[m * 256 : (m + 1) * 256, :], wq_v[g])
        rows = slice(m * 256, (m + 1) * 256)
        c, s = cos_v[rows, :] * scale, sin_v[rows, :] * scale
        for j in range(4):
            turned = turn(x[:, j * HEAD : (j + 1) * HEAD], c, s).astype(BF16)
            for k in range(4):
                q_v[(4 * m + k) * 2 + g, j * PART : (j + 1) * PART, :] = turned[
                    k * PART : (k + 1) * PART
                ]
        slot(n + 1)

    row = lax.rem(lax.broadcasted_iota(jnp.int32, (BODY, HEAD), 0), PART)
    col = lax.broadcasted_iota(jnp.int32, (BODY, HEAD), 1)
    diag = (col <= row, col <= row + PART)

    def in_turn(bodies, scores, finish):
        every = [scores(*body) for body in bodies]
        for body, s in zip(bodies, every):
            finish(*body, s)

    def bodies_of(t):
        start, size = TILES[t]
        return [(b, g) for g in range(2) for b in range(start // PART, (start + size) // PART)]

    def local_scores(b, g):
        keys = (b // 2 + 1) * HEAD
        return dot_t(q_v[b * 2 + g], kvl[0:keys, g * HEAD : (g + 1) * HEAD])

    def local_finish(b, g, s):
        before = b // 2 * HEAD
        last = jnp.where(diag[b % 2], s[:, before:], LOW)
        s = jnp.concatenate([s[:, :before], last], axis=1) if before else last
        top = jnp.max(s, axis=1, keepdims=True)
        p = jnp.exp(s - top).astype(BF16)
        ol[b * 2 + g] = dot(p, vl_aug[g, 0 : before + HEAD, :])
        ml[b * 2 + g] = jnp.broadcast_to(top, (BODY, HEAD))

    for t in range(1, len(TILES)):
        in_turn(bodies_of(t), local_scores, local_finish)
        slot(4 + t)

    got, eight = pl.ds(0, 6 * PIECE), pl.ds(0, 8 * PIECE)

    def anchor_here(ch):
        @pl.when(core == 1)
        def _():
            pltpu.make_async_copy(kva.at[got], kva.at[got], rest_recv.at[ch]).wait()

        @pl.when(core == 0)
        def _():
            pltpu.make_async_copy(kva.at[eight], kva.at[eight], rest_recv.at[ch]).wait()

        rows = pl.ds(ch * CROWS, CROWS)
        for g in range(2):
            va_aug[g, rows, 0:HEAD] = kva[rows, 256 + g * HEAD : 256 + (g + 1) * HEAD]

    def tile_rows(t):
        return pl.ds(*TILES[t])

    def ctx_copy(t):
        rows = tile_rows(t)
        return pltpu.make_async_remote_copy(
            src_ref=ctx.at[rows], dst_ref=ctx_sib.at[rows], send_sem=ctx_send,
            recv_sem=ctx_recv.at[t], device_id=sibling, device_id_type=MESH,
        )

    def x_copy(t, c):
        cols = pl.ds(c * 512, 512)
        return pltpu.make_async_remote_copy(
            src_ref=sbuf.at[tile_rows(t), cols], dst_ref=rbuf.at[tile_rows(t), cols],
            send_sem=x_send, recv_sem=x_recv.at[t],
            device_id=far, device_id_type=MESH,
        )

    has_anchor = blk > 0

    def early_scores(b, g):
        q, cols = q_v[b * 2 + g], slice(g * HEAD, (g + 1) * HEAD)
        return dot_t(q, kva[0:EARLY, cols]), dot_t(q, kvl[0:HEAD, cols])

    def early_finish(b, g, s):
        s = jnp.concatenate(
            [jnp.where(has_anchor, s[0], LOW), jnp.where(diag[b % 2], s[1], LOW)], axis=1
        )
        top = jnp.max(s, axis=1, keepdims=True)
        p = jnp.exp(s - top).astype(BF16)
        ol[b * 2 + g] = dot(p[:, 0:EARLY], va_aug[g, 0:EARLY, :]) + dot(
            p[:, EARLY:], vl_aug[g, 0:HEAD, :]
        )
        ml[b * 2 + g] = jnp.broadcast_to(top, (BODY, HEAD))

    for ch in range(CHUNKS - 1):
        anchor_here(ch)
    in_turn(bodies_of(0), early_scores, early_finish)
    anchor_here(CHUNKS - 1)

    def first_key(b):
        return 0 if b * PART >= TILES[0][1] else EARLY

    def anchor_scores(b, g):
        return dot_t(q_v[b * 2 + g], kva[first_key(b) :, g * HEAD : (g + 1) * HEAD])

    def anchor_finish(b, g, s):
        before = ml[b * 2 + g][:, 0:1]
        both = jnp.maximum(jnp.max(s, axis=1, keepdims=True), before)
        top = jnp.where(has_anchor, both, before)
        p = jnp.exp(s - jnp.where(has_anchor, both, -LOW)).astype(BF16)
        o = dot(p, va_aug[g, first_key(b) :, :]) + ol[b * 2 + g] * jnp.exp(before - top)
        res = (o[:, 0:HEAD] / o[:, HEAD:]).astype(BF16)
        for j in range(4):
            cols = slice((g * 4 + j) * HEAD, (g * 4 + j + 1) * HEAD)
            ctx[b * PART : (b + 1) * PART, cols] = res[j * PART : (j + 1) * PART]

    def anchor_tile(t):
        in_turn(bodies_of(t), anchor_scores, anchor_finish)
        ctx_copy(t).start()

    def near_part(start):
        rows = pl.ds(start, 256)
        acc_l[rows, :] = dot(ctx[rows, :], wo_a[1]) + dot(ctx_sib[rows, :], wo_b[1])

    def sibling_here(t):
        wait_all(ctx_sib.at[tile_rows(t)], ctx_recv.at[t])

    anchor_tile(0)
    wait_all(wo_a, load_sem.at[2])
    head_rows = tile_rows(0)
    acc_r[...] = dot(ctx[head_rows, :], wo_a[0])
    wait_all(wo_b, wob_recv)
    sibling_here(0)
    for c in range(2):
        cols = slice(c * 512, (c + 1) * 512)
        sbuf[head_rows, cols] = (
            acc_r[:, cols] + dot(ctx_sib[head_rows, :], wo_b[0, :, cols])
        ).astype(BF16)
        x_copy(0, c).start()
    def far_part(t):
        sibling_here(t)
        rows = tile_rows(t)
        for c in range(2):
            cols = slice(c * 512, (c + 1) * 512)
            sbuf[rows, cols] = (
                dot(ctx[rows, :], wo_a[0, :, cols]) + dot(ctx_sib[rows, :], wo_b[0, :, cols])
            ).astype(BF16)
            x_copy(t, c).start()

    for t in range(1, len(TILES)):
        anchor_tile(t)
        if t > 1:
            far_part(t - 1)
    far_part(len(TILES) - 1)
    for start in range(0, ROWS, 256):
        near_part(start)

    for t in range(len(TILES)):
        rows = tile_rows(t)
        wait_all(rbuf.at[rows], x_recv.at[t])
        out[rows, :] = (acc_l[rows, :] + rbuf[rows, :].astype(F32)).astype(BF16)

    wait_all(wo_b, wob_send)
    for grp, pieces in ((0, 8 * CHUNKS), (1, 6 * CHUNKS)):
        @pl.when(jnp.logical_and(blk == 0, core == grp))
        def _(pieces=pieces):
            wait_all(kva.at[pl.ds(0, pieces * PIECE)], first_send)

    @pl.when(core == 1)
    def _():
        for part in range(2):
            for side, pieces in ((0, 8 * CHUNKS), (1, 6 * CHUNKS)):
                @pl.when(jnp.logical_and(lines[1 - part] == 0, xl == side))
                def _(part=part, pieces=pieces):
                    wait_all(kva.at[pl.ds(0, pieces * PIECE)], ring_send.at[part])

        wait_all(hid_v.at[pl.ds(0, 14 * CHUNKS * PIECE // 8)], rest_send)

    wait_all(ctx, ctx_send)
    wait_all(sbuf, x_send)


def local(hidden_states, w_query, key_matrix, value_matrix, w_out):
    coarse_tab, fine_tab = rotary_tables(32)
    any_spec = pl.BlockSpec(memory_space=pl.ANY)
    dma = pltpu.SemaphoreType.DMA
    return pl.pallas_call(
        kernel,
        out_shape=pltpu.VMEM((ROWS, 1024), BF16),
        in_specs=[any_spec] * 7,
        out_specs=pl.BlockSpec(memory_space=pltpu.VMEM),
        scratch_shapes=[
            pltpu.VMEM((ROWS, WIDTH), BF16),
            pltpu.VMEM((2, WIDTH, 512), BF16),
            pltpu.VMEM((WIDTH, 512), BF16),
            pltpu.VMEM((2, 1024, 1024), BF16),
            pltpu.VMEM((2, 1024, 1024), BF16),
            pltpu.VMEM((2, ROWS // 16, HEAD), F32),
            pltpu.VMEM((2, 16, HEAD), F32),
            pltpu.VMEM((ROWS, HEAD), F32),
            pltpu.VMEM((ROWS, HEAD), F32),
            pltpu.VMEM((KROWS, 512), F32),
            pltpu.VMEM((ROWS, 512), BF16),
            pltpu.VMEM((ROWS, 512), BF16),
            pltpu.VMEM((ROWS, 512), BF16),
            pltpu.VMEM((PARTS * 2, BODY, HEAD), BF16),
            pltpu.VMEM((2, ROWS, 2 * HEAD), BF16),
            pltpu.VMEM((2, ROWS, 2 * HEAD), BF16),
            pltpu.VMEM((PARTS * 2, BODY, 2 * HEAD), F32),
            pltpu.VMEM((PARTS * 2, BODY, HEAD), F32),
            pltpu.VMEM((ROWS, 1024), BF16),
            pltpu.VMEM((ROWS, 1024), BF16),
            pltpu.VMEM((TILES[0][1], 1024), F32),
            pltpu.VMEM((ROWS, 1024), F32),
            pltpu.VMEM((ROWS, 1024), BF16),
            pltpu.VMEM((ROWS, 1024), BF16),
            dma((4,)), dma, dma,
            dma, dma((CHUNKS, 2)), dma((2,)), dma, dma((CHUNKS,)),
            dma, dma((len(TILES),)), dma, dma((len(TILES),)),
        ],
        compiler_params=pltpu.CompilerParams(
            collective_id=0, has_side_effects=True, vmem_limit_bytes=60 * 2**20
        ),
        name="layer",
    )(
        hidden_states, w_query, key_matrix, value_matrix, w_out,
        jnp.asarray(coarse_tab), jnp.asarray(fine_tab),
    )


def solution(mesh):
    in_specs = (P("blk", None), P(None, "head"), P(None, "head"), P(None, "head"), P("head", None))
    out_specs = P("blk", "head")
    return jax.shard_map(local, mesh=mesh, in_specs=in_specs, out_specs=out_specs, check_vma=False)
```
